128 devices in a mesh: wide: 16 (over z, y_lo, core), col: 8 (over y_hi, x).
Axes of the slice: x: 4, y: 4 (y_hi: 2, y_lo: 2; y = y_hi * 2 + y_lo), z: 4, core: 2. Of those that a mesh axis runs over, the one named last changes fastest.
Arguments:
- amplitudes: bfloat16 [1280, 65536], P('col', 'wide'), may hold values from -6 to 6
- integrals: bfloat16 [16, 16, 256, 12288], P(None, 'wide', None, 'col'), may hold values from -0.0234375 to 0.0234375
- tile_rows: int32 [256], replicated, may hold values from 64 to 256, as said below
Outputs:
- ladder: float32 [1280, 12288], P('wide', 'col')
The draws below stay inside these ranges and needn't reach their ends.
Inputs may be any that keep to these rules, and one draw needn't show every extreme that they name: `tile_rows`: tile 0 is full.
All inputs are finite; a program needn't handle non-finite values.
Results may differ from the reference program's by a relative error of at most 0.0003.
Values may be sent and summed in bfloat16 or wider, within the bound.
A program may use at most 128 MiB of HBM per device.

```python
import jax
import jax.numpy as jnp
from jax import lax

OCC_PAIRS = 1280
TILE = 256
TILES_DEV = 16
AB_DEV = 1536
PAIRS_CD = 65536
SLAB = 12288
N_WIDE = 16
N_COL = 8


def draw_tile_rows(key, part):
    key = jax.random.fold_in(key, 7)
    counts = jax.random.randint(key, (TILES_DEV * N_WIDE,), TILE // 4, TILE + 1).astype(jnp.int32)
    return counts.at[0].set(TILE)


def steps_of(own_key, dims, cuts, low, high):
    gain, own = 1.0, jax.random.fold_in(own_key, 6)
    for position, blocks in cuts:
        steps = jnp.exp(jax.random.uniform(jax.random.fold_in(own, position), (blocks,), jnp.float32, low / len(cuts), high / len(cuts)))
        gain = gain * jnp.repeat(steps, dims[position] // blocks).reshape([-1 if axis == position else 1 for axis in range(len(dims))])
    return gain


def normal_values(own_key, shape, width, bound, split=(), kind=jnp.bfloat16):
    level = steps_of(own_key, shape, split, -0.22, 0.18) if split else 1.0
    result = jax.random.normal(own_key, shape, jnp.float32) * width * level
    return jnp.minimum(jnp.maximum(result, -bound), bound).astype(kind)


def setup_inputs(seed: int = 0) -> dict:
    key_list = jax.random.split(jax.random.key(seed), 4)
    return {
        "amplitudes": normal_values(key_list[0], (OCC_PAIRS, PAIRS_CD), 1.0, 6.0, ((0, 8), (1, 16))),
        "integrals": normal_values(key_list[1], (TILES_DEV, N_WIDE, TILE, SLAB), PAIRS_CD ** -0.5, 0.0234375, ((1, 16), (3, 8))),
        "tile_rows": draw_tile_rows(jax.random.fold_in(key_list[3], 71), 0),
    }


def reference(amplitudes, integrals, tile_rows):
    live = (jnp.arange(TILE, dtype=jnp.int32)[None, :] < tile_rows[:, None]).reshape(PAIRS_CD)
    masked = amplitudes * live.astype(jnp.bfloat16)[None, :]
    flat = integrals.reshape(PAIRS_CD, SLAB)
    left = masked.astype(jnp.float32)

    def block(index):
        part = lax.dynamic_slice_in_dim(flat, index * AB_DEV, AB_DEV, 1).astype(jnp.float32)
        return jnp.dot(left, part, preferred_element_type=jnp.float32)

    pieces = lax.map(block, jnp.arange(N_COL, dtype=jnp.int32))
    return jnp.transpose(pieces, (1, 0, 2)).reshape(OCC_PAIRS, SLAB)
```

```python
import functools

import jax
import jax.numpy as jnp
from jax import lax
from jax.experimental import pallas as pl
from jax.experimental.pallas import tpu as pltpu
from jax.sharding import PartitionSpec as P

MESH = pl.DeviceIdType.MESH
SUB = 16
TILE = 256
TILES = 16
N_WIDE = 16
COLS = 8
BLOCK_N = 256


def kernel(
    chunks,
    counts_ref,
    amps_ref,
    ints_ref,
    out_ref,
    panel,
    flat,
    part,
    from_core,
    from_z,
    from_y,
    acc,
    own_sem,
    load_sem,
    a2a_send,
    a2a_recv,
    col_send,
    col_recv,
    red_send,
    red_recv,
):
    wide = lax.axis_index("wide")
    col = lax.axis_index("col")
    z, ylo, core = wide // 4, lax.rem(wide // 2, 2), lax.rem(wide, 2)
    yhi, x = col // 4, lax.rem(col, 4)

    def at_col(dy, dx):
        return lax.rem(yhi + dy, 2) * 4 + lax.rem(x + dx + 4, 4)

    def at_wide(dz, dy, dk):
        return lax.rem(z + dz + 4, 4) * 4 + lax.rem(ylo + dy, 2) * 2 + lax.rem(core + dk, 2)

    def peer(i):
        return lax.rem(z + i // 4, 4) * 4 + lax.rem(ylo + (i // 2) % 2, 2) * 2 + lax.rem(core + i % 2, 2)

    load = pltpu.make_async_copy(ints_ref, flat, load_sem)
    load.start()

    barrier = pltpu.get_barrier_semaphore()
    for i in range(1, N_WIDE):
        pl.semaphore_signal(barrier, 1, device_id=(peer(i), col), device_id_type=MESH)
    for c in (at_col(1, 0), at_col(0, 1), at_col(0, -1)):
        pl.semaphore_signal(barrier, 1, device_id=(wide, c), device_id_type=MESH)
    pl.semaphore_wait(barrier, N_WIDE - 1 + 3)

    def a2a_copy(t, i):
        to = peer(i)
        return pltpu.make_async_remote_copy(
            amps_ref.at[:, pl.ds(pl.multiple_of(t * SUB, SUB), SUB), pl.ds(pl.multiple_of(to * TILE, TILE), TILE)],
            panel.at[t, :, col, :, pl.ds(pl.multiple_of(wide * TILE, TILE), TILE)],
            a2a_send.at[t],
            a2a_recv.at[t],
            device_id=(to, col),
            device_id_type=MESH,
        )

    def own_copy(t):
        return pltpu.make_async_copy(
            amps_ref.at[:, pl.ds(pl.multiple_of(t * SUB, SUB), SUB), pl.ds(pl.multiple_of(wide * TILE, TILE), TILE)],
            panel.at[t, :, col, :, pl.ds(pl.multiple_of(wide * TILE, TILE), TILE)],
            own_sem.at[t],
        )

    def others(t):
        return panel.at[t, :, col, :, pl.ds(0, (N_WIDE - 1) * TILE)]

    def col_copy(t, slot):
        whole = lambda c: panel.at[t, :, c]
        half = lambda c, k: panel.at[t, k, c]
        ref, to = {
            0: lambda: (whole(col), at_col(1, 0)),
            1: lambda: (whole(col), at_col(0, 1)),
            2: lambda: (whole(col), at_col(0, -1)),
            3: lambda: (whole(at_col(1, 0)), at_col(0, 1)),
            4: lambda: (whole(at_col(1, 0)), at_col(0, -1)),
            5: lambda: (half(at_col(0, -1), 0), at_col(0, 1)),
            6: lambda: (half(at_col(0, 1), 1), at_col(0, -1)),
            7: lambda: (half(at_col(1, -1), 0), at_col(0, 1)),
            8: lambda: (half(at_col(1, 1), 1), at_col(0, -1)),
        }[slot]()
        return pltpu.make_async_remote_copy(
            ref, ref, col_send.at[t, slot], col_recv.at[t, slot], device_id=(wide, to), device_id_type=MESH
        )

    def core_copy(t):
        return pltpu.make_async_remote_copy(
            part.at[t, 1 - core],
            from_core.at[t],
            red_send.at[t, 0],
            red_recv.at[t, 0],
            device_id=(at_wide(0, 0, 1), col),
            device_id_type=MESH,
        )

    def z_copy(t, d):
        zo = lax.rem(z + d, 4)
        return pltpu.make_async_remote_copy(
            part.at[t, core, pl.ds(pl.multiple_of(zo * 2 * SUB, 2 * SUB), 2 * SUB)],
            from_z.at[t, d - 1],
            red_send.at[t, d],
            red_recv.at[t, d],
            device_id=(at_wide(d, 0, 0), col),
            device_id_type=MESH,
        )

    def y_copy(t):
        return pltpu.make_async_remote_copy(
            acc.at[t, 1 - ylo],
            from_y.at[t],
            red_send.at[t, 4],
            red_recv.at[t, 4],
            device_id=(at_wide(0, 1, 0), col),
            device_id_type=MESH,
        )

    def scatter(t):
        for i in range(1, N_WIDE):
            a2a_copy(t, i).start()
        own_copy(t).start()

    def mask_and_send(t):
        own_copy(t).wait()
        pltpu.make_async_copy(others(t), others(t), a2a_recv.at[t]).wait()
        for s in range(TILES):
            count = counts_ref[s * N_WIDE + wide]
            where = (t, slice(None), col, slice(None), slice(s * TILE, (s + 1) * TILE))
            live = lax.broadcasted_iota(jnp.int32, (2, SUB, TILE), 2) < count
            panel[where] = jnp.where(live, panel[where].astype(jnp.float32), 0.0).astype(jnp.bfloat16)
        for slot in (0, 1, 2):
            col_copy(t, slot).start()

    def matmul(t):

        @pl.loop(0, flat.shape[1] // BLOCK_N)
        def _(n):
            cols = pl.ds(pl.multiple_of(n * BLOCK_N, BLOCK_N), BLOCK_N)
            left = panel[t].reshape(2 * COLS * SUB, panel.shape[-1])
            res = jnp.dot(left, flat[:, cols], preferred_element_type=jnp.float32)
            part[t, :, :, cols] = res.reshape(2, COLS * SUB, BLOCK_N)

    def gathered(t):
        for slot in (5, 6, 7, 8):
            col_copy(t, slot).wait_recv()

    def core_sum(t):
        core_copy(t).wait_recv()
        part[t, core] = part[t, core] + from_core[t]
        for d in (2, 1, 3):
            z_copy(t, d).start()

    def z_sum(t):
        for d in (1, 2, 3):
            z_copy(t, d).wait_recv()
        rows = pl.ds(pl.multiple_of(z * 2 * SUB, 2 * SUB), 2 * SUB)
        total = part[t, core, rows] + from_z[t, 0] + from_z[t, 1] + from_z[t, 2]
        acc[t] = total.reshape(acc.shape[1:])
        y_copy(t).start()

    def y_sum(t):
        y_copy(t).wait_recv()
        out_ref[pl.ds(pl.multiple_of(t * SUB, SUB), SUB)] = acc[t, ylo] + from_y[t]

    scatter(0)
    scatter(1)
    mask_and_send(0)
    load.wait()

    @pl.loop(0, chunks + 1)
    def _(t):
        @pl.when(t < chunks)
        def _():
            col_copy(t, 0).wait_recv()
            col_copy(t, 3).start()
            col_copy(t, 4).start()
            col_copy(t, 1).wait_recv()
            col_copy(t, 5).start()
            col_copy(t, 2).wait_recv()
            col_copy(t, 6).start()

        @pl.when(t + 1 < chunks)
        def _():
            mask_and_send(t + 1)

        @pl.when(t + 2 < chunks)
        def _():
            scatter(t + 2)

        @pl.when(t >= 1)
        def _():
            gathered(t - 1)
            matmul(t - 1)
            core_copy(t - 1).start()

        @pl.when(t < chunks)
        def _():
            col_copy(t, 3).wait_recv()
            col_copy(t, 7).start()
            col_copy(t, 4).wait_recv()
            col_copy(t, 8).start()

        @pl.when(t >= 2)
        def _():
            z_sum(t - 2)

        @pl.when(t >= 1)
        def _():
            core_sum(t - 1)

        @pl.when(t >= 2)
        def _():
            y_sum(t - 2)

    z_sum(chunks - 1)
    y_sum(chunks - 1)

    @pl.loop(0, chunks)
    def _(t):
        pltpu.make_async_copy(others(t), others(t), a2a_send.at[t]).wait()
        for slot in range(9):
            col_copy(t, slot).wait_send()
        core_copy(t).wait_send()
        for d in (1, 2, 3):
            z_copy(t, d).wait_send()
        y_copy(t).wait_send()


def shards(amplitudes, integrals, tile_rows):
    rows, depth = amplitudes.shape
    chunks = rows // (2 * SUB)
    columns = integrals.shape[-1]
    f32, bf16 = jnp.float32, jnp.bfloat16
    dma = pltpu.SemaphoreType.DMA
    return pl.pallas_call(
        functools.partial(kernel, chunks),
        out_shape=jax.ShapeDtypeStruct((chunks * SUB, columns), f32),
        in_specs=[
            pl.BlockSpec(memory_space=pltpu.SMEM),
            pl.BlockSpec(memory_space=pltpu.VMEM),
            pl.BlockSpec(memory_space=pl.ANY),
        ],
        out_specs=pl.BlockSpec(memory_space=pltpu.VMEM),
        scratch_shapes=[
            pltpu.VMEM((chunks, 2, COLS, SUB, depth), bf16),
            pltpu.VMEM((depth, columns), bf16),
            pltpu.VMEM((chunks, 2, COLS * SUB, columns), f32),
            pltpu.VMEM((chunks, COLS * SUB, columns), f32),
            pltpu.VMEM((chunks, 3, 2 * SUB, columns), f32),
            pltpu.VMEM((chunks, SUB, columns), f32),
            pltpu.VMEM((chunks, 2, SUB, columns), f32),
            dma((chunks,)),
            dma,
            dma((chunks,)),
            dma((chunks,)),
            dma((chunks, 9)),
            dma((chunks, 9)),
            dma((chunks, 5)),
            dma((chunks, 5)),
        ],
        compiler_params=pltpu.CompilerParams(
            collective_id=0, has_side_effects=True, vmem_limit_bytes=60 * 2**20
        ),
        cost_estimate=pl.CostEstimate(
            flops=2 * COLS * rows * depth * columns, bytes_accessed=2 * depth * (rows + columns), transcendentals=0
        ),
        name="ladder",
    )(tile_rows, amplitudes.reshape(2, rows // 2, depth), integrals.reshape(depth, columns))


def solution(mesh):
    return jax.shard_map(
        shards,
        mesh=mesh,
        in_specs=(P("col", "wide"), P(None, "wide", None, "col"), P()),
        out_specs=P("wide", "col"),
        check_vma=False,
    )
```

```python
import functools

import jax
import jax.numpy as jnp
from jax import lax
from jax.experimental import pallas as pl
from jax.experimental.pallas import tpu as pltpu
from jax.sharding import PartitionSpec as P

MESH = pl.DeviceIdType.MESH
SUB = 16
TILE = 256
TILES = 16
N_WIDE = 16
COLS = 8
BLOCK_N = 256
LANES = 128
WINDOW = TILE + LANES
PER_WINDOW = WINDOW // LANES
WIDTHS = (2944, 3200)


def kernel(
    chunks,
    packed,
    counts_ref,
    amps_ref,
    ints_ref,
    out_ref,
    panel,
    flat,
    part,
    from_core,
    from_z,
    from_y,
    acc,
    own_sem,
    load_sem,
    a2a_send,
    a2a_recv,
    col_send,
    col_recv,
    red_send,
    red_recv,
    *pack_refs,
):
    if packed:
        arrived, raw, windows, offs, picks = pack_refs
    else:
        arrived, raw = None, flat
    wide = lax.axis_index("wide")
    col = lax.axis_index("col")
    z, ylo, core = wide // 4, lax.rem(wide // 2, 2), lax.rem(wide, 2)
    yhi, x = col // 4, lax.rem(col, 4)

    def at_col(dy, dx):
        return lax.rem(yhi + dy, 2) * 4 + lax.rem(x + dx + 4, 4)

    def at_wide(dz, dy, dk):
        return lax.rem(z + dz + 4, 4) * 4 + lax.rem(ylo + dy, 2) * 2 + lax.rem(core + dk, 2)

    def peer(i):
        return lax.rem(z + i // 4, 4) * 4 + lax.rem(ylo + (i // 2) % 2, 2) * 2 + lax.rem(core + i % 2, 2)

    load = pltpu.make_async_copy(ints_ref, raw, load_sem)
    load.start()

    barrier = pltpu.get_barrier_semaphore()
    for i in range(1, N_WIDE):
        pl.semaphore_signal(barrier, 1, device_id=(peer(i), col), device_id_type=MESH)
    for c in (at_col(1, 0), at_col(0, 1), at_col(0, -1)):
        pl.semaphore_signal(barrier, 1, device_id=(wide, c), device_id_type=MESH)
    pl.semaphore_wait(barrier, N_WIDE - 1 + 3)

    def landing(t, cols):
        if packed:
            return arrived.at[t, :, :, cols]
        return panel.at[t, :, col, :, cols]

    def a2a_copy(t, i):
        to = peer(i)
        return pltpu.make_async_remote_copy(
            amps_ref.at[:, pl.ds(pl.multiple_of(t * SUB, SUB), SUB), pl.ds(pl.multiple_of(to * TILE, TILE), TILE)],
            landing(t, pl.ds(pl.multiple_of(wide * TILE, TILE), TILE)),
            a2a_send.at[t],
            a2a_recv.at[t],
            device_id=(to, col),
            device_id_type=MESH,
        )

    def own_copy(t):
        return pltpu.make_async_copy(
            amps_ref.at[:, pl.ds(pl.multiple_of(t * SUB, SUB), SUB), pl.ds(pl.multiple_of(wide * TILE, TILE), TILE)],
            landing(t, pl.ds(pl.multiple_of(wide * TILE, TILE), TILE)),
            own_sem.at[t],
        )

    def others(t):
        return landing(t, pl.ds(0, (N_WIDE - 1) * TILE))

    def col_copy(t, slot):
        whole = lambda c: panel.at[t, :, c]
        half = lambda c, k: panel.at[t, k, c]
        ref, to = {
            0: lambda: (whole(col), at_col(1, 0)),
            1: lambda: (whole(col), at_col(0, 1)),
            2: lambda: (whole(col), at_col(0, -1)),
            3: lambda: (whole(at_col(1, 0)), at_col(0, 1)),
            4: lambda: (whole(at_col(1, 0)), at_col(0, -1)),
            5: lambda: (half(at_col(0, -1), 0), at_col(0, 1)),
            6: lambda: (half(at_col(0, 1), 1), at_col(0, -1)),
            7: lambda: (half(at_col(1, -1), 0), at_col(0, 1)),
            8: lambda: (half(at_col(1, 1), 1), at_col(0, -1)),
        }[slot]()
        return pltpu.make_async_remote_copy(
            ref, ref, col_send.at[t, slot], col_recv.at[t, slot], device_id=(wide, to), device_id_type=MESH
        )

    def core_copy(t):
        return pltpu.make_async_remote_copy(
            part.at[t, 1 - core],
            from_core.at[t],
            red_send.at[t, 0],
            red_recv.at[t, 0],
            device_id=(at_wide(0, 0, 1), col),
            device_id_type=MESH,
        )

    def z_copy(t, d):
        zo = lax.rem(z + d, 4)
        return pltpu.make_async_remote_copy(
            part.at[t, core, pl.ds(pl.multiple_of(zo * 2 * SUB, 2 * SUB), 2 * SUB)],
            from_z.at[t, d - 1],
            red_send.at[t, d],
            red_recv.at[t, d],
            device_id=(at_wide(d, 0, 0), col),
            device_id_type=MESH,
        )

    def y_copy(t):
        return pltpu.make_async_remote_copy(
            acc.at[t, 1 - ylo],
            from_y.at[t],
            red_send.at[t, 4],
            red_recv.at[t, 4],
            device_id=(at_wide(0, 1, 0), col),
            device_id_type=MESH,
        )

    def scatter(t):
        for i in range(1, N_WIDE):
            a2a_copy(t, i).start()
        own_copy(t).start()

    def count_of(s):
        return counts_ref[s * N_WIDE + wide]

    def mask(t):
        for s in range(TILES):
            where = (t, slice(None), col, slice(None), slice(s * TILE, (s + 1) * TILE))
            live = lax.broadcasted_iota(jnp.int32, (2, SUB, TILE), 2) < count_of(s)
            panel[where] = jnp.where(live, panel[where].astype(jnp.float32), 0.0).astype(jnp.bfloat16)

    def plan():
        start = jnp.int32(0)
        for s in range(TILES):
            offs[s] = start
            start = start + (((count_of(s) + (SUB - 1)) >> 4) << 4)
        offs[TILES] = start
        ends = [offs[s + 1] for s in range(TILES)]

        @pl.loop(0, panel.shape[-1] // LANES)
        def _(q):
            first = jnp.int32(0)
            for end in ends:
                first = first + jnp.where(end <= q * LANES, 1, 0)
            for d in range(3):
                s = jnp.minimum(first + d, TILES - 1)
                valid = (first + d < TILES) & (offs[s] < (q + 1) * LANES)
                picks[q * 3 + d] = jnp.where(valid, s * PER_WINDOW + q - (offs[s] >> 7), TILES * PER_WINDOW)

        windows[TILES * PER_WINDOW] = jnp.zeros(windows.shape[1:], windows.dtype)

    def pack(t):
        lane = lax.broadcasted_iota(jnp.int32, (2 * SUB, WINDOW), 1)
        pad = jnp.zeros((2 * SUB, LANES), jnp.float32)
        for s in range(TILES):
            phase = offs[s] & (LANES - 1)
            tile = arrived[t, :, :, s * TILE : (s + 1) * TILE].astype(jnp.float32).reshape(2 * SUB, TILE)
            turned = pltpu.roll(jnp.concatenate([tile, pad], axis=1), phase, 1)
            kept = jnp.where((lane >= phase) & (lane < phase + count_of(s)), turned, 0.0).astype(jnp.bfloat16)
            for b in range(PER_WINDOW):
                windows[s * PER_WINDOW + b] = kept[:, b * LANES : (b + 1) * LANES].reshape(2, SUB, LANES)
        for q in range(panel.shape[-1] // LANES):
            block = windows[picks[q * 3]] + windows[picks[q * 3 + 1]] + windows[picks[q * 3 + 2]]
            panel[t, :, col, :, q * LANES : (q + 1) * LANES] = block

    def pack_rows():
        @functools.partial(lax.fori_loop, 0, flat.shape[0] // SUB, init_val=(jnp.int32(0), jnp.int32(0)))
        def _(b, at):
            s, i = at
            flat[pl.ds(pl.multiple_of(b * SUB, SUB), SUB)] = raw[s * (TILE // SUB) + i]
            last = i + 1 >= ((count_of(s) + (SUB - 1)) >> 4)
            return jnp.where(last, jnp.minimum(s + 1, TILES - 1), s), jnp.where(last, 0, i + 1)

    def mask_and_send(t):
        own_copy(t).wait()
        pltpu.make_async_copy(others(t), others(t), a2a_recv.at[t]).wait()
        if packed:
            pack(t)
        else:
            mask(t)
        for slot in (0, 1, 2):
            col_copy(t, slot).start()

    def matmul(t):

        @pl.loop(0, flat.shape[1] // BLOCK_N)
        def _(n):
            cols = pl.ds(pl.multiple_of(n * BLOCK_N, BLOCK_N), BLOCK_N)
            left = panel[t].reshape(2 * COLS * SUB, panel.shape[-1])
            res = jnp.dot(left, flat[:, cols], preferred_element_type=jnp.float32)
            part[t, :, :, cols] = res.reshape(2, COLS * SUB, BLOCK_N)

    def gathered(t):
        for slot in (5, 6, 7, 8):
            col_copy(t, slot).wait_recv()

    def core_sum(t):
        core_copy(t).wait_recv()
        part[t, core] = part[t, core] + from_core[t]
        for d in (2, 1, 3):
            z_copy(t, d).start()

    def z_sum(t):
        for d in (1, 2, 3):
            z_copy(t, d).wait_recv()
        rows = pl.ds(pl.multiple_of(z * 2 * SUB, 2 * SUB), 2 * SUB)
        total = part[t, core, rows] + from_z[t, 0] + from_z[t, 1] + from_z[t, 2]
        acc[t] = total.reshape(acc.shape[1:])
        y_copy(t).start()

    def y_sum(t):
        y_copy(t).wait_recv()
        out_ref[pl.ds(pl.multiple_of(t * SUB, SUB), SUB)] = acc[t, ylo] + from_y[t]

    scatter(0)
    scatter(1)
    if packed:
        plan()
    mask_and_send(0)
    load.wait()
    if packed:
        pack_rows()

    @pl.loop(0, chunks + 1)
    def _(t):
        @pl.when(t < chunks)
        def _():
            col_copy(t, 0).wait_recv()
            col_copy(t, 3).start()
            col_copy(t, 4).start()
            col_copy(t, 1).wait_recv()
            col_copy(t, 5).start()
            col_copy(t, 2).wait_recv()
            col_copy(t, 6).start()

        @pl.when(t + 1 < chunks)
        def _():
            mask_and_send(t + 1)

        @pl.when(t + 2 < chunks)
        def _():
            scatter(t + 2)

        @pl.when(t >= 1)
        def _():
            gathered(t - 1)
            matmul(t - 1)
            core_copy(t - 1).start()

        @pl.when(t < chunks)
        def _():
            col_copy(t, 3).wait_recv()
            col_copy(t, 7).start()
            col_copy(t, 4).wait_recv()
            col_copy(t, 8).start()

        @pl.when(t >= 2)
        def _():
            z_sum(t - 2)

        @pl.when(t >= 1)
        def _():
            core_sum(t - 1)

        @pl.when(t >= 2)
        def _():
            y_sum(t - 2)

    z_sum(chunks - 1)
    y_sum(chunks - 1)

    @pl.loop(0, chunks)
    def _(t):
        pltpu.make_async_copy(others(t), others(t), a2a_send.at[t]).wait()
        for slot in range(9):
            col_copy(t, slot).wait_send()
        core_copy(t).wait_send()
        for d in (1, 2, 3):
            z_copy(t, d).wait_send()
        y_copy(t).wait_send()


def ladder(index, width, amplitudes, integrals, tile_rows):
    _, rows, depth = amplitudes.shape
    chunks = rows // SUB
    columns = integrals.shape[-1]
    packed = width < depth
    f32, bf16 = jnp.float32, jnp.bfloat16
    dma = pltpu.SemaphoreType.DMA
    pack_scratch = [
        pltpu.VMEM((chunks, 2, SUB, depth), bf16),
        pltpu.VMEM((depth // SUB, SUB, columns), bf16),
        pltpu.VMEM((TILES * PER_WINDOW + 1, 2, SUB, LANES), bf16),
        pltpu.SMEM((TILES + 1,), jnp.int32),
        pltpu.SMEM((3 * width // LANES,), jnp.int32),
    ]
    if packed:
        integrals = integrals.reshape(depth // SUB, SUB, columns)
    return pl.pallas_call(
        functools.partial(kernel, chunks, packed),
        out_shape=jax.ShapeDtypeStruct((rows, columns), f32),
        in_specs=[
            pl.BlockSpec(memory_space=pltpu.SMEM),
            pl.BlockSpec(memory_space=pltpu.VMEM),
            pl.BlockSpec(memory_space=pl.ANY),
        ],
        out_specs=pl.BlockSpec(memory_space=pltpu.VMEM),
        scratch_shapes=[
            pltpu.VMEM((chunks, 2, COLS, SUB, width), bf16),
            pltpu.VMEM((width, columns), bf16),
            pltpu.VMEM((chunks, 2, COLS * SUB, columns), f32),
            pltpu.VMEM((chunks, COLS * SUB, columns), f32),
            pltpu.VMEM((chunks, 3, 2 * SUB, columns), f32),
            pltpu.VMEM((chunks, SUB, columns), f32),
            pltpu.VMEM((chunks, 2, SUB, columns), f32),
            dma((chunks,)),
            dma,
            dma((chunks,)),
            dma((chunks,)),
            dma((chunks, 9)),
            dma((chunks, 9)),
            dma((chunks, 5)),
            dma((chunks, 5)),
            *(pack_scratch if packed else []),
        ],
        compiler_params=pltpu.CompilerParams(
            collective_id=index, has_side_effects=True, vmem_limit_bytes=60 * 2**20
        ),
        cost_estimate=pl.CostEstimate(
            flops=4 * COLS * rows * width * columns,
            bytes_accessed=2 * depth * (2 * rows + columns),
            transcendentals=0,
        ),
        name=f"ladder_{width}",
    )(tile_rows, amplitudes, integrals)


def shards(amplitudes, integrals, tile_rows):
    rows, depth = amplitudes.shape
    amplitudes = amplitudes.reshape(2, rows // 2, depth)
    integrals = integrals.reshape(depth, integrals.shape[-1])
    padded = (tile_rows + (SUB - 1)) // SUB * SUB
    need = jnp.max(jnp.sum(padded.reshape(TILES, N_WIDE), axis=0))
    widths = (*WIDTHS, depth)
    which = sum((need > width).astype(jnp.int32) for width in WIDTHS)
    branches = [functools.partial(ladder, i, width) for i, width in enumerate(widths)]
    return lax.switch(which, branches, amplitudes, integrals, tile_rows)


def solution(mesh):
    return jax.shard_map(
        shards,
        mesh=mesh,
        in_specs=(P("col", "wide"), P(None, "wide", None, "col"), P()),
        out_specs=P("wide", "col"),
        check_vma=False,
    )
```

```python
import functools

import jax
import jax.numpy as jnp
from jax import lax
from jax.experimental import pallas as pl
from jax.experimental.pallas import tpu as pltpu
from jax.sharding import PartitionSpec as P

MESH = pl.DeviceIdType.MESH
SUB = 16
TILE = 256
TILES = 16
N_WIDE = 16
COLS = 8
BLOCK_N = 256
LANES = 128
WINDOW = TILE + LANES
PER_WINDOW = WINDOW // LANES
PIECES = 2
WIDTHS = (2944, 3072, 3200, 3328)


def kernel(
    chunks,
    packed,
    counts_ref,
    amps_ref,
    ints_ref,
    out_ref,
    panel,
    flat,
    part,
    from_core,
    from_z,
    from_y,
    acc,
    own_sem,
    load_sem,
    a2a_send,
    a2a_recv,
    col_send,
    col_recv,
    red_send,
    red_recv,
    *pack_refs,
):
    if packed:
        arrived, raw, windows, offs, picks = pack_refs
    else:
        arrived, raw = None, flat
    wide = lax.axis_index("wide")
    col = lax.axis_index("col")
    z, ylo, core = wide // 4, lax.rem(wide // 2, 2), lax.rem(wide, 2)
    yhi, x = col // 4, lax.rem(col, 4)

    def at_col(dy, dx):
        return lax.rem(yhi + dy, 2) * 4 + lax.rem(x + dx + 4, 4)

    def at_wide(dz, dy, dk):
        return lax.rem(z + dz + 4, 4) * 4 + lax.rem(ylo + dy, 2) * 2 + lax.rem(core + dk, 2)

    def peer(i):
        return lax.rem(z + i // 4, 4) * 4 + lax.rem(ylo + (i // 2) % 2, 2) * 2 + lax.rem(core + i % 2, 2)

    load = pltpu.make_async_copy(ints_ref, raw, load_sem)
    load.start()

    barrier = pltpu.get_barrier_semaphore()
    for i in range(1, N_WIDE):
        pl.semaphore_signal(barrier, 1, device_id=(peer(i), col), device_id_type=MESH)
    for c in (at_col(1, 0), at_col(0, 1), at_col(0, -1)):
        pl.semaphore_signal(barrier, 1, device_id=(wide, c), device_id_type=MESH)
    pl.semaphore_wait(barrier, N_WIDE - 1 + 3)

    def landing(t, cols):
        if packed:
            return arrived.at[t, :, :, cols]
        return panel.at[t, :, col, :, cols]

    def a2a_copy(t, i):
        to = peer(i)
        return pltpu.make_async_remote_copy(
            amps_ref.at[:, pl.ds(pl.multiple_of(t * SUB, SUB), SUB), pl.ds(pl.multiple_of(to * TILE, TILE), TILE)],
            landing(t, pl.ds(pl.multiple_of(wide * TILE, TILE), TILE)),
            a2a_send.at[t],
            a2a_recv.at[t],
            device_id=(to, col),
            device_id_type=MESH,
        )

    def own_copy(t):
        return pltpu.make_async_copy(
            amps_ref.at[:, pl.ds(pl.multiple_of(t * SUB, SUB), SUB), pl.ds(pl.multiple_of(wide * TILE, TILE), TILE)],
            landing(t, pl.ds(pl.multiple_of(wide * TILE, TILE), TILE)),
            own_sem.at[t],
        )

    def others(t):
        return landing(t, pl.ds(0, (N_WIDE - 1) * TILE))

    def col_copy(t, slot):
        whole = lambda c: panel.at[t, :, c]
        half = lambda c, k: panel.at[t, k, c]
        ref, to = {
            0: lambda: (whole(col), at_col(1, 0)),
            1: lambda: (whole(col), at_col(0, 1)),
            2: lambda: (whole(col), at_col(0, -1)),
            3: lambda: (whole(at_col(1, 0)), at_col(0, 1)),
            4: lambda: (whole(at_col(1, 0)), at_col(0, -1)),
            5: lambda: (half(at_col(0, -1), 0), at_col(0, 1)),
            6: lambda: (half(at_col(0, 1), 1), at_col(0, -1)),
            7: lambda: (half(at_col(1, -1), 0), at_col(0, 1)),
            8: lambda: (half(at_col(1, 1), 1), at_col(0, -1)),
        }[slot]()
        return pltpu.make_async_remote_copy(
            ref, ref, col_send.at[t, slot], col_recv.at[t, slot], device_id=(wide, to), device_id_type=MESH
        )

    def core_copy(t, p):
        return pltpu.make_async_remote_copy(
            part.at[t, p, 1 - core],
            from_core.at[t, p],
            red_send.at[t, p * 5],
            red_recv.at[t, p * 5],
            device_id=(at_wide(0, 0, 1), col),
            device_id_type=MESH,
        )

    def z_copy(t, p, d):
        zo = lax.rem(z + d, 4)
        return pltpu.make_async_remote_copy(
            part.at[t, p, core, pl.ds(pl.multiple_of(zo * 2 * SUB, 2 * SUB), 2 * SUB)],
            from_z.at[t, p, d - 1],
            red_send.at[t, p * 5 + d],
            red_recv.at[t, p * 5 + d],
            device_id=(at_wide(d, 0, 0), col),
            device_id_type=MESH,
        )

    def y_copy(t, p):
        return pltpu.make_async_remote_copy(
            acc.at[t, p, 1 - ylo],
            from_y.at[t, p],
            red_send.at[t, p * 5 + 4],
            red_recv.at[t, p * 5 + 4],
            device_id=(at_wide(0, 1, 0), col),
            device_id_type=MESH,
        )

    def scatter(t):
        for i in range(1, N_WIDE):
            a2a_copy(t, i).start()
        own_copy(t).start()

    def count_of(s):
        return counts_ref[s * N_WIDE + wide]

    def mask(t):
        for s in range(TILES):
            where = (t, slice(None), col, slice(None), slice(s * TILE, (s + 1) * TILE))
            live = lax.broadcasted_iota(jnp.int32, (2, SUB, TILE), 2) < count_of(s)
            panel[where] = jnp.where(live, panel[where].astype(jnp.float32), 0.0).astype(jnp.bfloat16)

    def plan():
        start = jnp.int32(0)
        for s in range(TILES):
            offs[s] = start
            start = start + (((count_of(s) + (SUB - 1)) >> 4) << 4)
        offs[TILES] = start
        ends = [offs[s + 1] for s in range(TILES)]

        @pl.loop(0, panel.shape[-1] // LANES)
        def _(q):
            first = jnp.int32(0)
            for end in ends:
                first = first + jnp.where(end <= q * LANES, 1, 0)
            for d in range(3):
                s = jnp.minimum(first + d, TILES - 1)
                valid = (first + d < TILES) & (offs[s] < (q + 1) * LANES)
                picks[q * 3 + d] = jnp.where(valid, s * PER_WINDOW + q - (offs[s] >> 7), TILES * PER_WINDOW)

        windows[TILES * PER_WINDOW] = jnp.zeros(windows.shape[1:], windows.dtype)

    def pack(t):
        lane = lax.broadcasted_iota(jnp.int32, (2 * SUB, WINDOW), 1)
        pad = jnp.zeros((2 * SUB, LANES), jnp.float32)
        for s in range(TILES):
            phase = offs[s] & (LANES - 1)
            tile = arrived[t, :, :, s * TILE : (s + 1) * TILE].astype(jnp.float32).reshape(2 * SUB, TILE)
            turned = pltpu.roll(jnp.concatenate([tile, pad], axis=1), phase, 1)
            kept = jnp.where((lane >= phase) & (lane < phase + count_of(s)), turned, 0.0).astype(jnp.bfloat16)
            for b in range(PER_WINDOW):
                windows[s * PER_WINDOW + b] = kept[:, b * LANES : (b + 1) * LANES].reshape(2, SUB, LANES)
        for q in range(panel.shape[-1] // LANES):
            block = windows[picks[q * 3]] + windows[picks[q * 3 + 1]] + windows[picks[q * 3 + 2]]
            panel[t, :, col, :, q * LANES : (q + 1) * LANES] = block

    def pack_rows():
        @functools.partial(lax.fori_loop, 0, flat.shape[0] // SUB, init_val=(jnp.int32(0), jnp.int32(0)))
        def _(b, at):
            s, i = at
            flat[pl.ds(pl.multiple_of(b * SUB, SUB), SUB)] = raw[s * (TILE // SUB) + i]
            last = i + 1 >= ((count_of(s) + (SUB - 1)) >> 4)
            return jnp.where(last, jnp.minimum(s + 1, TILES - 1), s), jnp.where(last, 0, i + 1)

    def mask_and_send(t):
        own_copy(t).wait()
        pltpu.make_async_copy(others(t), others(t), a2a_recv.at[t]).wait()
        if packed:
            pack(t)
        else:
            mask(t)
        for slot in (0, 1, 2):
            col_copy(t, slot).start()

    def matmul(t):
        left = panel[t].reshape(2 * COLS * SUB, panel.shape[-1])
        piece = part.shape[-1]
        for p in range(PIECES):
            for n in range(0, piece, BLOCK_N):
                cols = slice(p * piece + n, p * piece + n + BLOCK_N)
                res = jnp.dot(left, flat[:, cols], preferred_element_type=jnp.float32)
                part[t, p, :, :, n : n + BLOCK_N] = res.reshape(2, COLS * SUB, BLOCK_N)
            core_copy(t, p).start()

    def gathered(t):
        for slot in (5, 6, 7, 8):
            col_copy(t, slot).wait_recv()

    def core_sum(t):
        for p in range(PIECES):
            core_copy(t, p).wait_recv()
            part[t, p, core] = part[t, p, core] + from_core[t, p]
            for d in (2, 1, 3):
                z_copy(t, p, d).start()

    def z_sum(t):
        rows = pl.ds(pl.multiple_of(z * 2 * SUB, 2 * SUB), 2 * SUB)
        for p in range(PIECES):
            for d in (1, 2, 3):
                z_copy(t, p, d).wait_recv()
            total = part[t, p, core, rows] + from_z[t, p, 0] + from_z[t, p, 1] + from_z[t, p, 2]
            acc[t, p] = total.reshape(acc.shape[2:])
            y_copy(t, p).start()

    def y_sum(t):
        piece = part.shape[-1]
        for p in range(PIECES):
            y_copy(t, p).wait_recv()
            out_ref[pl.ds(pl.multiple_of(t * SUB, SUB), SUB), p * piece : (p + 1) * piece] = acc[t, p, ylo] + from_y[t, p]

    scatter(0)
    scatter(1)
    if packed:
        plan()
    mask_and_send(0)
    load.wait()
    if packed:
        pack_rows()

    @pl.loop(0, chunks + 1)
    def _(t):
        @pl.when(t < chunks)
        def _():
            col_copy(t, 0).wait_recv()
            col_copy(t, 3).start()
            col_copy(t, 4).start()
            col_copy(t, 1).wait_recv()
            col_copy(t, 5).start()
            col_copy(t, 2).wait_recv()
            col_copy(t, 6).start()

        @pl.when(t + 1 < chunks)
        def _():
            mask_and_send(t + 1)

        @pl.when(t + 2 < chunks)
        def _():
            scatter(t + 2)

        @pl.when(t >= 1)
        def _():
            gathered(t - 1)
            matmul(t - 1)

        @pl.when(t < chunks)
        def _():
            col_copy(t, 3).wait_recv()
            col_copy(t, 7).start()
            col_copy(t, 4).wait_recv()
            col_copy(t, 8).start()

        @pl.when(t >= 1)
        def _():
            core_sum(t - 1)

        @pl.when(t >= 2)
        def _():
            z_sum(t - 2)

        @pl.when(t >= 3)
        def _():
            y_sum(t - 3)

    z_sum(chunks - 1)
    y_sum(chunks - 2)
    y_sum(chunks - 1)

    @pl.loop(0, chunks)
    def _(t):
        pltpu.make_async_copy(others(t), others(t), a2a_send.at[t]).wait()
        for slot in range(9):
            col_copy(t, slot).wait_send()
        for p in range(PIECES):
            core_copy(t, p).wait_send()
            for d in (1, 2, 3):
                z_copy(t, p, d).wait_send()
            y_copy(t, p).wait_send()


def ladder(index, width, amplitudes, integrals, tile_rows):
    _, rows, depth = amplitudes.shape
    chunks = rows // SUB
    columns = integrals.shape[-1]
    piece = columns // PIECES
    packed = width < depth
    f32, bf16 = jnp.float32, jnp.bfloat16
    dma = pltpu.SemaphoreType.DMA
    pack_scratch = [
        pltpu.VMEM((chunks, 2, SUB, depth), bf16),
        pltpu.VMEM((depth // SUB, SUB, columns), bf16),
        pltpu.VMEM((TILES * PER_WINDOW + 1, 2, SUB, LANES), bf16),
        pltpu.SMEM((TILES + 1,), jnp.int32),
        pltpu.SMEM((3 * width // LANES,), jnp.int32),
    ]
    if packed:
        integrals = integrals.reshape(depth // SUB, SUB, columns)
    return pl.pallas_call(
        functools.partial(kernel, chunks, packed),
        out_shape=jax.ShapeDtypeStruct((rows, columns), f32),
        in_specs=[
            pl.BlockSpec(memory_space=pltpu.SMEM),
            pl.BlockSpec(memory_space=pltpu.VMEM),
            pl.BlockSpec(memory_space=pl.ANY),
        ],
        out_specs=pl.BlockSpec(memory_space=pltpu.VMEM),
        scratch_shapes=[
            pltpu.VMEM((chunks, 2, COLS, SUB, width), bf16),
            pltpu.VMEM((width, columns), bf16),
            pltpu.VMEM((chunks, PIECES, 2, COLS * SUB, piece), f32),
            pltpu.VMEM((chunks, PIECES, COLS * SUB, piece), f32),
            pltpu.VMEM((chunks, PIECES, 3, 2 * SUB, piece), f32),
            pltpu.VMEM((chunks, PIECES, SUB, piece), f32),
            pltpu.VMEM((chunks, PIECES, 2, SUB, piece), f32),
            dma((chunks,)),
            dma,
            dma((chunks,)),
            dma((chunks,)),
            dma((chunks, 9)),
            dma((chunks, 9)),
            dma((chunks, 5 * PIECES)),
            dma((chunks, 5 * PIECES)),
            *(pack_scratch if packed else []),
        ],
        compiler_params=pltpu.CompilerParams(
            collective_id=index, has_side_effects=True, vmem_limit_bytes=60 * 2**20
        ),
        cost_estimate=pl.CostEstimate(
            flops=4 * COLS * rows * width * columns,
            bytes_accessed=2 * depth * (2 * rows + columns),
            transcendentals=0,
        ),
        name=f"ladder_{width}",
    )(tile_rows, amplitudes, integrals)


def shards(amplitudes, integrals, tile_rows):
    rows, depth = amplitudes.shape
    amplitudes = amplitudes.reshape(2, rows // 2, depth)
    integrals = integrals.reshape(depth, integrals.shape[-1])
    padded = (tile_rows + (SUB - 1)) // SUB * SUB
    need = jnp.max(jnp.sum(padded.reshape(TILES, N_WIDE), axis=0))
    widths = (*WIDTHS, depth)
    which = sum((need > width).astype(jnp.int32) for width in WIDTHS)
    branches = [functools.partial(ladder, i, width) for i, width in enumerate(widths)]
    return lax.switch(which, branches, amplitudes, integrals, tile_rows)


def solution(mesh):
    return jax.shard_map(
        shards,
        mesh=mesh,
        in_specs=(P("col", "wide"), P(None, "wide", None, "col"), P()),
        out_specs=P("wide", "col"),
        check_vma=False,
    )
```

```python
import functools

import jax
import jax.numpy as jnp
from jax import lax
from jax.experimental import pallas as pl
from jax.experimental.pallas import tpu as pltpu
from jax.sharding import PartitionSpec as P

MESH = pl.DeviceIdType.MESH
SUB = 16
TILE = 256
TILES = 16
N_WIDE = 16
COLS = 8
BLOCK_N = 256
FAR_FIRST = (8, 9, 10, 11, 4, 5, 6, 7, 12, 13, 14, 15, 2, 3, 1)
LANES = 128
WINDOW = TILE + LANES
PER_WINDOW = WINDOW // LANES
PIECES = 3
WIDTHS = (2944, 3072, 3200, 3328)


def kernel(
    chunks,
    packed,
    counts_ref,
    amps_ref,
    ints_ref,
    out_ref,
    panel,
    flat,
    part,
    from_core,
    from_z,
    from_y,
    acc,
    own_sem,
    load_sem,
    a2a_send,
    a2a_recv,
    col_send,
    col_recv,
    red_send,
    red_recv,
    *pack_refs,
):
    if packed:
        arrived, raw, windows, offs, picks = pack_refs
    else:
        arrived, raw = None, flat
    wide = lax.axis_index("wide")
    col = lax.axis_index("col")
    z, ylo, core = wide // 4, lax.rem(wide // 2, 2), lax.rem(wide, 2)
    yhi, x = col // 4, lax.rem(col, 4)

    def at_col(dy, dx):
        return lax.rem(yhi + dy, 2) * 4 + lax.rem(x + dx + 4, 4)

    def at_wide(dz, dy, dk):
        return lax.rem(z + dz + 4, 4) * 4 + lax.rem(ylo + dy, 2) * 2 + lax.rem(core + dk, 2)

    def peer(i):
        return lax.rem(z + i // 4, 4) * 4 + lax.rem(ylo + (i // 2) % 2, 2) * 2 + lax.rem(core + i % 2, 2)

    load = pltpu.make_async_copy(ints_ref, raw, load_sem)
    load.start()

    barrier = pltpu.get_barrier_semaphore()
    for i in range(1, N_WIDE):
        pl.semaphore_signal(barrier, 1, device_id=(peer(i), col), device_id_type=MESH)
    for c in (at_col(1, 0), at_col(0, 1), at_col(0, -1)):
        pl.semaphore_signal(barrier, 1, device_id=(wide, c), device_id_type=MESH)
    pl.semaphore_wait(barrier, N_WIDE - 1 + 3)

    def landing(t, cols):
        if packed:
            return arrived.at[t, :, :, cols]
        return panel.at[t, :, col, :, cols]

    def a2a_copy(t, i):
        to = peer(i)
        return pltpu.make_async_remote_copy(
            amps_ref.at[:, pl.ds(pl.multiple_of(t * SUB, SUB), SUB), pl.ds(pl.multiple_of(to * TILE, TILE), TILE)],
            landing(t, pl.ds(pl.multiple_of(wide * TILE, TILE), TILE)),
            a2a_send.at[t],
            a2a_recv.at[t],
            device_id=(to, col),
            device_id_type=MESH,
        )

    def own_copy(t):
        return pltpu.make_async_copy(
            amps_ref.at[:, pl.ds(pl.multiple_of(t * SUB, SUB), SUB), pl.ds(pl.multiple_of(wide * TILE, TILE), TILE)],
            landing(t, pl.ds(pl.multiple_of(wide * TILE, TILE), TILE)),
            own_sem.at[t],
        )

    def others(t):
        return landing(t, pl.ds(0, (N_WIDE - 1) * TILE))

    def col_copy(t, slot):
        whole = lambda c: panel.at[t, :, c]
        half = lambda c, k: panel.at[t, k, c]
        ref, to = {
            0: lambda: (whole(col), at_col(1, 0)),
            1: lambda: (whole(col), at_col(0, 1)),
            2: lambda: (whole(col), at_col(0, -1)),
            3: lambda: (whole(at_col(1, 0)), at_col(0, 1)),
            4: lambda: (whole(at_col(1, 0)), at_col(0, -1)),
            5: lambda: (half(at_col(0, -1), 0), at_col(0, 1)),
            6: lambda: (half(at_col(0, 1), 1), at_col(0, -1)),
            7: lambda: (half(at_col(1, -1), 0), at_col(0, 1)),
            8: lambda: (half(at_col(1, 1), 1), at_col(0, -1)),
        }[slot]()
        return pltpu.make_async_remote_copy(
            ref, ref, col_send.at[t, slot], col_recv.at[t, slot], device_id=(wide, to), device_id_type=MESH
        )

    def core_copy(t, p):
        return pltpu.make_async_remote_copy(
            part.at[t, p, 1 - core],
            from_core.at[t, p],
            red_send.at[t, p * 5],
            red_recv.at[t, p * 5],
            device_id=(at_wide(0, 0, 1), col),
            device_id_type=MESH,
        )

    def z_copy(t, p, d):
        zo = lax.rem(z + d, 4)
        return pltpu.make_async_remote_copy(
            part.at[t, p, core, pl.ds(pl.multiple_of(zo * 2 * SUB, 2 * SUB), 2 * SUB)],
            from_z.at[t, p, d - 1],
            red_send.at[t, p * 5 + d],
            red_recv.at[t, p * 5 + d],
            device_id=(at_wide(d, 0, 0), col),
            device_id_type=MESH,
        )

    def y_copy(t, p):
        return pltpu.make_async_remote_copy(
            acc.at[t, p, 1 - ylo],
            from_y.at[t, p],
            red_send.at[t, p * 5 + 4],
            red_recv.at[t, p * 5 + 4],
            device_id=(at_wide(0, 1, 0), col),
            device_id_type=MESH,
        )

    def scatter(t):
        for i in FAR_FIRST:
            a2a_copy(t, i).start()
        own_copy(t).start()

    def count_of(s):
        return counts_ref[s * N_WIDE + wide]

    def mask(t):
        for s in range(TILES):
            where = (t, slice(None), col, slice(None), slice(s * TILE, (s + 1) * TILE))
            live = lax.broadcasted_iota(jnp.int32, (2, SUB, TILE), 2) < count_of(s)
            panel[where] = jnp.where(live, panel[where].astype(jnp.float32), 0.0).astype(jnp.bfloat16)

    def plan():
        start = jnp.int32(0)
        for s in range(TILES):
            offs[s] = start
            start = start + (((count_of(s) + (SUB - 1)) >> 4) << 4)
        offs[TILES] = start
        ends = [offs[s + 1] for s in range(TILES)]

        @pl.loop(0, panel.shape[-1] // LANES)
        def _(q):
            first = jnp.int32(0)
            for end in ends:
                first = first + jnp.where(end <= q * LANES, 1, 0)
            for d in range(3):
                s = jnp.minimum(first + d, TILES - 1)
                valid = (first + d < TILES) & (offs[s] < (q + 1) * LANES)
                picks[q * 3 + d] = jnp.where(valid, s * PER_WINDOW + q - (offs[s] >> 7), TILES * PER_WINDOW)

        windows[TILES * PER_WINDOW] = jnp.zeros(windows.shape[1:], windows.dtype)

    def pack(t):
        lane = lax.broadcasted_iota(jnp.int32, (2 * SUB, WINDOW), 1)
        pad = jnp.zeros((2 * SUB, LANES), jnp.float32)
        for s in range(TILES):
            phase = offs[s] & (LANES - 1)
            tile = arrived[t, :, :, s * TILE : (s + 1) * TILE].astype(jnp.float32).reshape(2 * SUB, TILE)
            turned = pltpu.roll(jnp.concatenate([tile, pad], axis=1), phase, 1)
            kept = jnp.where((lane >= phase) & (lane < phase + count_of(s)), turned, 0.0).astype(jnp.bfloat16)
            for b in range(PER_WINDOW):
                windows[s * PER_WINDOW + b] = kept[:, b * LANES : (b + 1) * LANES].reshape(2, SUB, LANES)
        for q in range(panel.shape[-1] // LANES):
            block = windows[picks[q * 3]] + windows[picks[q * 3 + 1]] + windows[picks[q * 3 + 2]]
            panel[t, :, col, :, q * LANES : (q + 1) * LANES] = block

    def pack_rows():
        @functools.partial(lax.fori_loop, 0, flat.shape[0] // SUB, init_val=(jnp.int32(0), jnp.int32(0)))
        def _(b, at):
            s, i = at
            flat[pl.ds(pl.multiple_of(b * SUB, SUB), SUB)] = raw[s * (TILE // SUB) + i]
            last = i + 1 >= ((count_of(s) + (SUB - 1)) >> 4)
            return jnp.where(last, jnp.minimum(s + 1, TILES - 1), s), jnp.where(last, 0, i + 1)

    def mask_and_send(t):
        own_copy(t).wait()
        pltpu.make_async_copy(others(t), others(t), a2a_recv.at[t]).wait()
        if packed:
            pack(t)
        else:
            mask(t)
        for slot in (0, 1, 2):
            col_copy(t, slot).start()

    def matmul(t):
        left = panel[t].reshape(2 * COLS * SUB, panel.shape[-1])
        piece = part.shape[-1]
        for p in range(PIECES):
            for n in range(0, piece, BLOCK_N):
                cols = slice(p * piece + n, p * piece + n + BLOCK_N)
                res = jnp.dot(left, flat[:, cols], preferred_element_type=jnp.float32)
                part[t, p, :, :, n : n + BLOCK_N] = res.reshape(2, COLS * SUB, BLOCK_N)
            core_copy(t, p).start()

    def gathered(t):
        for slot in (5, 6, 7, 8):
            col_copy(t, slot).wait_recv()

    def core_sum(t):
        for p in range(PIECES):
            core_copy(t, p).wait_recv()
            part[t, p, core] = part[t, p, core] + from_core[t, p]
            for d in (2, 1, 3):
                z_copy(t, p, d).start()

    def z_sum(t):
        rows = pl.ds(pl.multiple_of(z * 2 * SUB, 2 * SUB), 2 * SUB)
        for p in range(PIECES):
            for d in (1, 2, 3):
                z_copy(t, p, d).wait_recv()
            total = part[t, p, core, rows] + from_z[t, p, 0] + from_z[t, p, 1] + from_z[t, p, 2]
            acc[t, p] = total.reshape(acc.shape[2:])
            y_copy(t, p).start()

    def y_sum(t):
        piece = part.shape[-1]
        for p in range(PIECES):
            y_copy(t, p).wait_recv()
            out_ref[pl.ds(pl.multiple_of(t * SUB, SUB), SUB), p * piece : (p + 1) * piece] = acc[t, p, ylo] + from_y[t, p]

    scatter(0)
    if packed:
        plan()
    scatter(1)
    mask_and_send(0)
    load.wait()
    if packed:
        pack_rows()

    @pl.loop(0, chunks + 1)
    def _(t):
        @pl.when(t < chunks)
        def _():
            col_copy(t, 0).wait_recv()
            col_copy(t, 3).start()
            col_copy(t, 4).start()
            col_copy(t, 1).wait_recv()
            col_copy(t, 5).start()
            col_copy(t, 2).wait_recv()
            col_copy(t, 6).start()

        @pl.when(t + 1 < chunks)
        def _():
            mask_and_send(t + 1)

        @pl.when(t + 2 < chunks)
        def _():
            scatter(t + 2)

        @pl.when(t >= 1)
        def _():
            gathered(t - 1)
            matmul(t - 1)

        @pl.when(t < chunks)
        def _():
            col_copy(t, 3).wait_recv()
            col_copy(t, 7).start()
            col_copy(t, 4).wait_recv()
            col_copy(t, 8).start()

        @pl.when(t >= 1)
        def _():
            core_sum(t - 1)

        @pl.when(t >= 2)
        def _():
            z_sum(t - 2)

        @pl.when(t >= 3)
        def _():
            y_sum(t - 3)

    z_sum(chunks - 1)
    y_sum(chunks - 2)
    y_sum(chunks - 1)

    @pl.loop(0, chunks)
    def _(t):
        pltpu.make_async_copy(others(t), others(t), a2a_send.at[t]).wait()
        for slot in range(9):
            col_copy(t, slot).wait_send()
        for p in range(PIECES):
            core_copy(t, p).wait_send()
            for d in (1, 2, 3):
                z_copy(t, p, d).wait_send()
            y_copy(t, p).wait_send()


def ladder(index, width, amplitudes, integrals, tile_rows):
    _, rows, depth = amplitudes.shape
    chunks = rows // SUB
    columns = integrals.shape[-1]
    piece = columns // PIECES
    packed = width < depth
    f32, bf16 = jnp.float32, jnp.bfloat16
    dma = pltpu.SemaphoreType.DMA
    pack_scratch = [
        pltpu.VMEM((chunks, 2, SUB, depth), bf16),
        pltpu.VMEM((depth // SUB, SUB, columns), bf16),
        pltpu.VMEM((TILES * PER_WINDOW + 1, 2, SUB, LANES), bf16),
        pltpu.SMEM((TILES + 1,), jnp.int32),
        pltpu.SMEM((3 * width // LANES,), jnp.int32),
    ]
    if packed:
        integrals = integrals.reshape(depth // SUB, SUB, columns)
    return pl.pallas_call(
        functools.partial(kernel, chunks, packed),
        out_shape=jax.ShapeDtypeStruct((rows, columns), f32),
        in_specs=[
            pl.BlockSpec(memory_space=pltpu.SMEM),
            pl.BlockSpec(memory_space=pltpu.VMEM),
            pl.BlockSpec(memory_space=pl.ANY),
        ],
        out_specs=pl.BlockSpec(memory_space=pltpu.VMEM),
        scratch_shapes=[
            pltpu.VMEM((chunks, 2, COLS, SUB, width), bf16),
            pltpu.VMEM((width, columns), bf16),
            pltpu.VMEM((chunks, PIECES, 2, COLS * SUB, piece), f32),
            pltpu.VMEM((chunks, PIECES, COLS * SUB, piece), f32),
            pltpu.VMEM((chunks, PIECES, 3, 2 * SUB, piece), f32),
            pltpu.VMEM((chunks, PIECES, SUB, piece), f32),
            pltpu.VMEM((chunks, PIECES, 2, SUB, piece), f32),
            dma((chunks,)),
            dma,
            dma((chunks,)),
            dma((chunks,)),
            dma((chunks, 9)),
            dma((chunks, 9)),
            dma((chunks, 5 * PIECES)),
            dma((chunks, 5 * PIECES)),
            *(pack_scratch if packed else []),
        ],
        compiler_params=pltpu.CompilerParams(
            collective_id=index, has_side_effects=True, vmem_limit_bytes=60 * 2**20
        ),
        cost_estimate=pl.CostEstimate(
            flops=4 * COLS * rows * width * columns,
            bytes_accessed=2 * depth * (2 * rows + columns),
            transcendentals=0,
        ),
        name=f"ladder_{width}",
    )(tile_rows, amplitudes, integrals)


def shards(amplitudes, integrals, tile_rows):
    rows, depth = amplitudes.shape
    amplitudes = amplitudes.reshape(2, rows // 2, depth)
    integrals = integrals.reshape(depth, integrals.shape[-1])
    padded = (tile_rows + (SUB - 1)) // SUB * SUB
    need = jnp.max(jnp.sum(padded.reshape(TILES, N_WIDE), axis=0))
    widths = (*WIDTHS, depth)
    which = sum((need > width).astype(jnp.int32) for width in WIDTHS)
    branches = [functools.partial(ladder, i, width) for i, width in enumerate(widths)]
    return lax.switch(which, branches, amplitudes, integrals, tile_rows)


def solution(mesh):
    return jax.shard_map(
        shards,
        mesh=mesh,
        in_specs=(P("col", "wide"), P(None, "wide", None, "col"), P()),
        out_specs=P("wide", "col"),
        check_vma=False,
    )
```
